256 devices in a mesh: gx: 16 (over z, core), gy: 16 (over y, x).
Axes of the slice: x: 4, y: 4, z: 8, core: 2. Of those that a mesh axis runs over, the one named last changes fastest.
Arguments:
- rhs: float32 [128, 128, 6, 3, 256], P('gx', 'gy'), may hold values from -400 to 400
- contrast: float32 [128, 128, 256], P('gx', 'gy'), may hold values from 0.2 to 2
- occupied: int32 [128, 128], P('gx', 'gy'), may hold values 0 or 1
- near: bfloat16 [5, 768, 768], replicated, may hold values from -0.078125 to 0.078125
- basis: bfloat16 [768, 64], replicated, may hold values from -0.21875 to 0.21875
- transfer: float32 [5, 4, 64, 64], replicated, may hold values from -0.5 to 0.5
- coupling: float32 [6, 20, 64, 64], replicated, may hold values from -0.15625 to 0.15625
Outputs:
- third: float32 [128, 128, 6, 3, 256], P('gx', 'gy')
- hess: float32 [6, 6], replicated
The draws below stay inside these ranges and needn't reach their ends.
All inputs are finite; a program needn't handle non-finite values. No bound on the sum of `occupied` on one device may be relied on, other than what follows from the above.
Results may differ from the reference program's by a relative error of at most 0.0031.
Values may be sent and summed in bfloat16 or wider, within the bound.
No kernel may reach another device: no remote copies, remote signals or barrier semaphores. Data moves between devices by JAX's collectives and lax.ppermute only.
A program may use at most 128 MiB of HBM per device.

```python
import math
import jax
import jax.numpy as jnp
from jax import lax

P_SIZE = 256
R = 64
NRHS = 6
NLX = 128
NLY = 128
LEVELS = 6


def draw_rhs(key, part):
    key_base = jax.random.fold_in(key, 11)
    key_values, key_box, key_voxel = jax.random.split(key_base, 3)
    shape_all = (NLX, NLY, NRHS, 3, P_SIZE)
    values_drawn = jnp.clip(jax.random.normal(key_values, shape_all, jnp.float32), -4.0, 4.0)
    box_scale = jnp.exp(math.log(10.0) * jax.random.uniform(key_box, (NLX, NLY), jnp.float32))
    rising = 1.0 + 2.0 * jnp.arange(NLX, dtype=jnp.float32) / NLX
    voxel_scale = jnp.exp(math.log(3.0) * jax.random.uniform(key_voxel, (P_SIZE,), jnp.float32))
    return values_drawn * (box_scale * rising[:, None])[:, :, None, None, None] * voxel_scale


def touch_ends(drawn, own_key, low, largest):
    spot = [jax.random.randint(jax.random.fold_in(own_key, axis), (), 0, length) for axis, length in enumerate(drawn.shape)]
    widest = drawn.shape.index(max(drawn.shape))
    next_to = spot[:widest] + [(spot[widest] + 1) % drawn.shape[widest]] + spot[widest + 1:]
    return drawn.at[tuple(spot)].set(low).at[tuple(next_to)].set(largest)


def levels(rng, dims, pieces, least, largest):
    loudness, own = 1.0, jax.random.fold_in(rng, 6)
    for axis_at, blocks in pieces:
        steps = jnp.exp(jax.random.uniform(jax.random.fold_in(own, axis_at), (blocks,), jnp.float32, least / len(pieces), largest / len(pieces)))
        loudness = loudness * jnp.repeat(steps, dims[axis_at] // blocks).reshape([-1 if axis == axis_at else 1 for axis in range(len(dims))])
    return loudness


def gaussian(stream_key, extent, scale, bound, kind=jnp.bfloat16):
    return jnp.clip(scale * jax.random.normal(stream_key, extent, jnp.float32), -bound, bound).astype(kind)


def setup_inputs(seed: int = 0) -> dict:
    keys = jax.random.split(jax.random.key(seed), 8)
    return {
        "rhs": draw_rhs(jax.random.fold_in(keys[7], 71), 0),
        "contrast": jnp.clip(jnp.exp(math.log(2.0) - 2.3025851 * jax.random.uniform(keys[1], (NLX, NLY, P_SIZE), jnp.float32) ** levels(keys[1], (NLX, NLY, P_SIZE), ((0, 16), (1, 16)), -0.2, 0.2)), 0.2, 2.0),
        "occupied": touch_ends((jax.random.randint(keys[2], (NLX, NLY), 0, 4) < 3).astype(jnp.int32), jax.random.fold_in(keys[2], 1), 0, 1),
        "near": gaussian(keys[3], (5, 3 * P_SIZE, 3 * P_SIZE), (27 * P_SIZE) ** -0.5, 0.078125),
        "basis": gaussian(keys[4], (3 * P_SIZE, R), (3 * P_SIZE) ** -0.5, 0.21875),
        "transfer": gaussian(keys[5], (LEVELS - 1, 4, R, R), (2 * R) ** -0.5, 0.5, jnp.float32),
        "coupling": gaussian(keys[6], (LEVELS, 20, R, R), (27 * R) ** -0.5, 0.15625, jnp.float32),
    }


PRECISE = lax.Precision.HIGHEST
EPSILON = 1e-06
NEAR_BASE = ((0, 0), (1, -1), (1, 0), (1, 1), (0, 1))

def near_terms():
    listing = []
    for slot_index, (shift_x, shift_y) in enumerate(NEAR_BASE):
        listing.append((shift_x, shift_y, slot_index, False))
        if shift_x != 0 or shift_y != 0:
            listing.append((-shift_x, -shift_y, slot_index, True))
    return listing

def far_terms():
    base_list = []
    for shift_x in range(-3, 4):
        for shift_y in range(-3, 4):
            if max(abs(shift_x), abs(shift_y)) >= 2 and (shift_x > 0 or (shift_x == 0 and shift_y > 0)):
                base_list.append((shift_x, shift_y))
    listing = []
    for slot_index, (shift_x, shift_y) in enumerate(base_list):
        listing.append((shift_x, shift_y, slot_index, False))
        listing.append((-shift_x, -shift_y, slot_index, True))
    return listing

def parent_close(parity, offset):
    return jnp.abs((parity + offset) // 2) <= 1

def lift(skeleton, matrices):
    size_x, size_y, fields, rank = skeleton.shape
    fold_x = 2 if size_x > 1 else 1
    fold_y = 2 if size_y > 1 else 1
    blocks = skeleton.reshape(size_x // fold_x, fold_x, size_y // fold_y, fold_y, fields, rank)
    total = jnp.zeros((size_x // fold_x, size_y // fold_y, fields, rank), jnp.float32)
    for child_x in range(fold_x):
        for child_y in range(fold_y):
            piece = blocks[:, child_x, :, child_y].reshape(-1, rank)
            total = total + jnp.dot(piece, matrices[2 * child_x + child_y], precision=PRECISE).reshape(total.shape)
    return total

def lower(parent, matrices, size_x, size_y):
    par_x, par_y, fields, rank = parent.shape
    fold_x = size_x // par_x
    fold_y = size_y // par_y
    flat_parent = parent.reshape(-1, rank)
    rows_list = []
    for child_x in range(fold_x):
        cols_list = []
        for child_y in range(fold_y):
            cols_list.append(jnp.dot(flat_parent, matrices[2 * child_x + child_y].T, precision=PRECISE).reshape(parent.shape))
        rows_list.append(jnp.stack(cols_list, axis=2))
    return jnp.stack(rows_list, axis=1).reshape(size_x, size_y, fields, rank)

def couple_padded(padded, size_x, size_y, matrices):
    fields, rank = (padded.shape[2], padded.shape[3])
    parity_x = jnp.arange(size_x, dtype=jnp.int32) % 2
    parity_y = jnp.arange(size_y, dtype=jnp.int32) % 2
    total = jnp.zeros((size_x, size_y, fields, rank), jnp.float32)
    for shift_x, shift_y, slot_index, flipped in far_terms():
        block = matrices[slot_index].T if flipped else matrices[slot_index]
        piece = padded[3 + shift_x:3 + shift_x + size_x, 3 + shift_y:3 + shift_y + size_y].reshape(-1, rank)
        keep = (parent_close(parity_x, shift_x)[:, None] & parent_close(parity_y, shift_y)[None, :]).astype(jnp.float32)
        total = total + keep[:, :, None, None] * jnp.dot(piece, block, precision=PRECISE).reshape(size_x, size_y, fields, rank)
    return total

def couple(skeleton, matrices):
    padded = jnp.pad(skeleton, ((3, 3), (3, 3), (0, 0), (0, 0)))
    return couple_padded(padded, skeleton.shape[0], skeleton.shape[1], matrices)

def apply_operator(field, occupied, contrast, near, basis, transfer, coupling):
    source = (occupied.astype(jnp.float32)[:, :, None, None, None] * contrast[:, :, None, None, :] * field).astype(jnp.bfloat16)
    size_x, size_y, fields = (source.shape[0], source.shape[1], source.shape[2])
    width = source.shape[3] * source.shape[4]
    rank = basis.shape[1]
    flat_source = source.reshape(size_x, size_y, fields, width)
    padded = jnp.pad(flat_source, ((1, 1), (1, 1), (0, 0), (0, 0)))
    near_sum = jnp.zeros((size_x, size_y, fields, width), jnp.float32)
    for shift_x, shift_y, slot_index, flipped in near_terms():
        block = near[slot_index].T if flipped else near[slot_index]
        piece = padded[1 + shift_x:1 + shift_x + size_x, 1 + shift_y:1 + shift_y + size_y].reshape(-1, width)
        near_sum = near_sum + jnp.dot(piece, block, preferred_element_type=jnp.float32).reshape(size_x, size_y, fields, width)
    skeleton = [jnp.dot(flat_source.reshape(-1, width), basis, preferred_element_type=jnp.float32).reshape(size_x, size_y, fields, rank)]
    for depth in range(LEVELS - 1):
        skeleton.append(lift(skeleton[-1], transfer[depth]))
    down = couple(skeleton[LEVELS - 1], coupling[LEVELS - 1])
    for depth in range(LEVELS - 2, -1, -1):
        child = skeleton[depth]
        down = couple(child, coupling[depth]) + lower(down, transfer[depth], child.shape[0], child.shape[1])
    far_part = jnp.dot(down.reshape(-1, rank), basis.T.astype(jnp.float32), precision=PRECISE).reshape(size_x, size_y, fields, width)
    return field + (near_sum + far_part).reshape(field.shape)

def reference(rhs, contrast, occupied, near, basis, transfer, coupling):

    def inner(first_arr, second_arr):
        return lax.optimization_barrier(jnp.mean(first_arr * second_arr, axis=(0, 1, 3, 4)))

    def spread(values):
        return values[None, None, :, None, None]

    def operate(field):
        return apply_operator(field, occupied, contrast, near, basis, transfer, coupling)
    scale_start = jnp.sqrt(inner(rhs, rhs) + EPSILON)
    first = rhs / spread(scale_start)
    image = operate(first)
    coef_first = inner(first, image)
    rest = image - spread(coef_first) * first
    norm_first = jnp.sqrt(inner(rest, rest) + EPSILON)
    second = rest / spread(norm_first)
    image = operate(second)
    coef_cross = inner(first, image)
    coef_second = inner(second, image)
    rest = image - spread(coef_cross) * first - spread(coef_second) * second
    norm_second = jnp.sqrt(inner(rest, rest) + EPSILON)
    third = rest / spread(norm_second)
    hess = jnp.stack([scale_start, coef_first, norm_first, coef_cross, coef_second, norm_second], axis=1)
    return (third, hess)
```

```python
import functools

import jax
import jax.numpy as jnp
from jax import lax
from jax.experimental import pallas as pl
from jax.experimental.pallas import tpu as pltpu
from jax.sharding import Mesh
from jax.sharding import PartitionSpec as P

F32, BF16 = jnp.float32, jnp.bfloat16
GX = ("z", "c")
GY = ("y", "x1", "x0")
CLASS_ORDER = ("c", "x0", "z", "y", "x1")
EVERYONE = ("z", "c", "y", "x1", "x0")
EPSILON = 1e-06
EXACT = lax.Precision.HIGHEST
HALF = ((1, -1), (1, 0), (1, 1), (0, 1))
AROUND = HALF + tuple((-a, -b) for a, b in HALF)
NEAR_SLOT = {(0, 0): 0, (1, -1): 1, (1, 0): 2, (1, 1): 3, (0, 1): 4}
FAR = [
    (dx, dy)
    for dx in range(-3, 4)
    for dy in range(-3, 4)
    if max(abs(dx), abs(dy)) >= 2 and (dx > 0 or (dx == 0 and dy > 0))
]
VMEM = pl.BlockSpec(memory_space=pltpu.VMEM)
SMEM = pl.BlockSpec(memory_space=pltpu.SMEM)
CHILDREN = [(c, e) for c in range(2) for e in range(2)]
PARENTS = (4, 2, 1)


def dot(a, b):
    return jnp.dot(a, b, preferred_element_type=F32)


def dot_t(a, b, precision=None):
    return lax.dot_general(
        a, b, (((1,), (1,)), ((), ())), preferred_element_type=F32, precision=precision
    )


def call(kernel, outs, specs, scratch, flops, *args):
    moved = sum(a.size * a.dtype.itemsize for a in args)
    return pl.pallas_call(
        kernel,
        out_shape=outs,
        in_specs=specs,
        out_specs=jax.tree.map(lambda _: VMEM, outs),
        scratch_shapes=scratch,
        compiler_params=pltpu.CompilerParams(vmem_limit_bytes=50 * 2**20),
        cost_estimate=pl.CostEstimate(flops=flops, bytes_accessed=moved, transcendentals=0),
    )(*args)


def pair_blocks(coupling_ref, inner_ref, high_ref, low_ref):
    zero = jnp.zeros((64, 64), F32)
    for level in range(6):
        flipped = {}
        for n, (dp, dq) in enumerate(HALF):
            for c_in, e_in in CHILDREN:
                for c in range(2):
                    row = []
                    for e in range(2):
                        d = (2 * dp + c_in - c, 2 * dq + e_in - e)
                        if max(abs(d[0]), abs(d[1])) < 2:
                            row.append(zero)
                        elif d in FAR:
                            row.append(coupling_ref[level, FAR.index(d)])
                        else:
                            k = FAR.index((-d[0], -d[1]))
                            if k not in flipped:
                                flipped[k] = coupling_ref[level, k].T
                            row.append(flipped[k])
                    r0 = (2 * c_in + e_in) * 64
                    rows, lanes = slice(r0, r0 + 64), slice(c * 128, c * 128 + 128)
                    block = jnp.concatenate(row, axis=1)
                    high = block.astype(BF16)
                    if level < 3:
                        inner_ref[level, n, rows, lanes] = high
                    else:
                        high_ref[level - 3, n, rows, lanes] = high
                        low_ref[level - 3, n, rows, lanes] = (block - high.astype(F32)).astype(BF16)


def in_two(x):
    high = x.astype(BF16)
    return high, (x - high.astype(F32)).astype(BF16)


def couple(x, pairs, level, k):
    high, low = in_two(x)
    product = dot if k < 4 else dot_t
    both = product(jnp.concatenate([high, low], axis=0), pairs[0][level, k % 4])
    out = both[0 : x.shape[0]] + both[x.shape[0] :]
    if len(pairs) > 1:
        out = out + product(high, pairs[1][level, k % 4])
    return out


def weight_rows(contrast_ref, occupied_ref, i):
    square = (8, 8)
    here = jnp.broadcast_to(occupied_ref[i : i + 1, :].astype(F32), square)
    same = lax.broadcasted_iota(jnp.int32, square, 0) == lax.broadcasted_iota(jnp.int32, square, 1)
    occupied = jnp.sum(jnp.where(same, here, 0.0), axis=1, keepdims=True)
    w = occupied * contrast_ref[8 * i : 8 * i + 8, :]
    return jnp.concatenate([jnp.concatenate([w] * 6, axis=0)] * 3, axis=1)


def lanes_to_one(x):
    total = x[:, 0:128]
    for k in range(1, x.shape[1] // 128):
        total = total + x[:, 128 * k : 128 * k + 128]
    return total


def field_row(sums):
    lane = lax.broadcasted_iota(jnp.int32, (1, 128), 1)
    row = jnp.zeros((1, 128), F32)
    for n, acc in enumerate(sums):
        for f in range(6):
            row = row + jnp.where(lane == 6 * n + f, jnp.sum(acc[8 * f : 8 * f + 8, :]), 0.0)
    return row


def left_half(shape):
    return lax.broadcasted_iota(jnp.int32, shape, len(shape) - 1) < 64


def tiles(ref, rows):
    return jnp.concatenate([ref[t, rows, :] for t in range(ref.shape[0])], axis=1)


def spread_skeleton(field_at, sums_row, refs, skel):
    contrast_ref, occupied_ref, basis_ref, transfer_ref = refs[0]
    src_ref, up_ref, down_ref, pay_ref, *tree = refs[1]
    twice = jnp.concatenate([basis_ref[...]] * 2, axis=0)
    for i in range(8):
        rows = slice(48 * i, 48 * i + 48)
        s = (weight_rows(contrast_ref, occupied_ref, i) * field_at(i)).astype(BF16)
        for t in range(6):
            src_ref[t, rows, :] = s[:, 128 * t : 128 * t + 128].astype(F32)
        skel[rows, :] = dot_t(s, twice)
        if i == 0:
            down_ref[:, 0:768] = s
        if i == 7:
            up_ref[:, 0:768] = s
    half = left_half((6, 128))
    for level, n in enumerate(PARENTS):
        node = tree[level]
        node[...] = jnp.zeros(node.shape, F32)
        offset = min(level, 1)
        for i in range(2 * n):
            for q in range(n):
                at = 48 * i + offset + 2 * q
                node[i % 2, pl.ds((i // 2 + 1) * 48 + 1 + q, 6, stride=8), :] = jnp.where(
                    half, skel[pl.ds(at, 6, stride=8), :], skel[pl.ds(at + 1, 6, stride=8), :]
                )
        lanes = slice(768 + 256 * level, 1024 + 256 * level)
        up_ref[:, lanes] = tiles(node, slice(48 * n, 48 * n + 48)).astype(BF16)
        down_ref[:, lanes] = tiles(node, slice(48, 96)).astype(BF16)
        skel[0 : 48 * n, :] = jnp.dot(
            tiles(node, slice(48, 48 * n + 48)),
            transfer_ref[level],
            precision=EXACT,
            preferred_element_type=F32,
        )
    top = skel[pl.ds(1, 6, stride=8), :]
    pay = jnp.concatenate([jnp.where(half[0:3], top[0:3, :], top[3:6, :]), sums_row], axis=0)
    pay_ref[...] = jnp.broadcast_to(pay[None], pay_ref.shape)


SOURCE_OUTS = [
    jax.ShapeDtypeStruct((6, 384, 128), F32),
    jax.ShapeDtypeStruct((48, 1536), BF16),
    jax.ShapeDtypeStruct((48, 1536), BF16),
    jax.ShapeDtypeStruct((256, 4, 128), F32),
    jax.ShapeDtypeStruct((2, 288, 128), F32),
    jax.ShapeDtypeStruct((2, 192, 128), F32),
    jax.ShapeDtypeStruct((2, 144, 128), F32),
]
SOURCE_SCRATCH = [pltpu.VMEM((384, 128), F32)]


def first_source(x_ref, contrast_ref, occupied_ref, basis_ref, transfer_ref, *rest):
    outs, skel = rest[:7], rest[7]
    acc = jnp.zeros((48, 128), F32)
    for i in range(8):
        x = x_ref[48 * i : 48 * i + 48, :]
        acc = acc + lanes_to_one(x * x)
    spread_skeleton(
        lambda i: x_ref[48 * i : 48 * i + 48, :],
        field_row([acc]),
        ((contrast_ref, occupied_ref, basis_ref, transfer_ref), outs),
        skel,
    )


def columns(pos_ref, src_ref, a0, a1, a2, above_ref, below_ref, left_ref, right_ref, above, below):
    gx = pos_ref[0]
    for t in range(12):
        lanes = slice(128 * t, 128 * t + 128)
        above[t] = above_ref[:, lanes].astype(F32) * (gx > 0).astype(F32)
        below[t] = below_ref[:, lanes].astype(F32) * (gx < 15).astype(F32)
    for out, side in ((left_ref, 0), (right_ref, 1)):
        j = 7 * side
        for t in range(6):
            out[0:60, 128 * t : 128 * t + 128] = jnp.concatenate(
                [
                    above[t, pl.ds(j, 6, stride=8), :],
                    src_ref[t, pl.ds(j, 48, stride=8), :],
                    below[t, pl.ds(j, 6, stride=8), :],
                ],
                axis=0,
            ).astype(BF16)
            out[60:80, 128 * t : 128 * t + 128] = jnp.zeros((20, 128), BF16)
        for t in range(2):
            parts = []
            for level, (node, n) in enumerate(zip((a0, a1, a2), PARENTS)):
                q = n if side else 1
                parts += [
                    above[6 + 2 * level + t, pl.ds(q, 6, stride=8), :],
                    node[t, pl.ds(48 + q, 6 * n, stride=8), :],
                    below[6 + 2 * level + t, pl.ds(q, 6, stride=8), :],
                ]
            parts.append(jnp.zeros((2, 128), F32))
            out[:, 768 + 128 * t : 896 + 128 * t] = jnp.concatenate(parts, axis=0).astype(BF16)


def near_and_low(
    pos_ref, src_ref, a0, a1, a2, above_ref, below_ref, left_ref, right_ref, near_ref, inner_ref,
    near_out, o0, o1, o2, wide, moved, edge, placed, n0, n1, n2, turned,
):
    gx, gy = pos_ref[0], pos_ref[1]
    up = (gx > 0).astype(F32)
    down = (gx < 15).astype(F32)
    for t in range(6):
        lanes = slice(128 * t, 128 * t + 128)
        wide[t, 0:48, :] = above_ref[:, lanes].astype(F32) * up
        wide[t, 48:432, :] = src_ref[t]
        wide[t, 432:480, :] = below_ref[:, lanes].astype(F32) * down
    flags = ((gy > 0).astype(F32), (gy < 15).astype(F32))
    first = True
    for b in (0, -1, 1):
        side_ref, flag = ((left_ref, flags[0]), (right_ref, flags[1]))[b > 0]
        if b != 0:
            edge[...] = side_ref[:, 0:768].astype(F32) * flag
        for t in range(6):
            lanes = slice(128 * t, 128 * t + 128)
            if b == 0:
                placed[:, lanes] = wide[t].astype(BF16)
                continue
            if b < 0:
                moved[t, 1:480, :] = wide[t, 0:479, :]
                moved[t, pl.ds(0, 60, stride=8), :] = edge[0:60, lanes]
            else:
                moved[t, 0:479, :] = wide[t, 1:480, :]
                moved[t, pl.ds(7, 60, stride=8), :] = edge[0:60, lanes]
            placed[:, lanes] = moved[t].astype(BF16)
        for a in (-1, 0, 1):
            lhs = placed[48 * (1 + a) : 48 * (1 + a) + 384, :]
            if (a, b) in NEAR_SLOT:
                part = dot(lhs, near_ref[NEAR_SLOT[a, b]])
            else:
                part = dot_t(lhs, near_ref[NEAR_SLOT[-a, -b]])
            if first:
                near_out[...] = part
                first = False
            else:
                near_out[...] += part
    start = 0
    for level, (node, full, out, n) in enumerate(
        zip((a0, a1, a2), (n0, n1, n2), (o0, o1, o2), PARENTS)
    ):
        size, lanes = 48 * (n + 2), slice(768 + 256 * level, 1024 + 256 * level)
        for t in range(2):
            lane = slice(lanes.start + 128 * t, lanes.start + 128 * t + 128)
            full[t] = node[t]
            full[t, 0:48, :] = above_ref[:, lane].astype(F32) * up
            full[t, size - 48 : size, :] = below_ref[:, lane].astype(F32) * down
        for side_ref, flag, q in ((left_ref, flags[0], 0), (right_ref, flags[1], n + 1)):
            edge[:, 0:256] = side_ref[:, 768:1024].astype(F32) * flag
            for t in range(2):
                full[t, pl.ds(q, 6 * (n + 2), stride=8), :] = edge[
                    start : start + 6 * (n + 2), 128 * t : 128 * t + 128
                ]
        total = jnp.zeros((48 * n, 256), F32)
        for dq in (-1, 0, 1):
            for t in range(2):
                lane = slice(128 * t, 128 * t + 128)
                if dq == 0:
                    turned[0:size, lane] = full[t]
                elif dq < 0:
                    turned[1:size, lane] = full[t, 0 : size - 1, :]
                    turned[0:1, lane] = full[t, 0:1, :]
                else:
                    turned[0 : size - 1, lane] = full[t, 1:size, :]
                    turned[size - 1 : size, lane] = full[t, 0:1, :]
            for k, (dp, dq_k) in enumerate(AROUND):
                if dq_k == dq:
                    lhs = turned[48 * (1 + dp) : 48 * (1 + dp) + 48 * n, :]
                    total = total + couple(lhs, (inner_ref,), level, k)
        out[...] = total
        start += 6 * (n + 2)


def lane_of(f):
    return (f % 3) * 128 + (f // 3) * 64


def select(chosen, table):
    high, low = in_two(table)
    return dot(chosen, high) + dot(chosen, low)


def far_above(pos_ref, all_ref, pairs, transfer_ref, by_child, grown, side_by):
    gx, gy = pos_ref[0], pos_ref[1]
    table = jnp.concatenate([all_ref[pl.ds(m, 256, stride=4), :] for m in range(3)], axis=1)
    classes = table
    row = lax.broadcasted_iota(jnp.int32, (32, 1), 0)
    around, child = row % 8, row // 8
    shift_p = sum(jnp.where(around == k, dp, 0) for k, (dp, _) in enumerate(AROUND))
    shift_q = sum(jnp.where(around == k, dq, 0) for k, (_, dq) in enumerate(AROUND))
    outs = []
    for step in range(3):
        n = 16 >> step
        at_p, at_q = (gx >> (step + 1)) + shift_p, (gy >> (step + 1)) + shift_q
        inside = (at_p >= 0) & (at_p < n // 2) & (at_q >= 0) & (at_q < n // 2)
        if step == 0:
            where = child * (n * n // 4) + at_p * (n // 2) + at_q
        else:
            where = (2 * at_p + child // 2) * n + 2 * at_q + child % 2
        lane = lax.broadcasted_iota(jnp.int32, (32, n * n), 1)
        chosen = ((lane == where) & inside).astype(F32).astype(BF16)
        picked = select(chosen, table)
        by_child[...] = jnp.zeros(by_child.shape, F32)
        for f in range(6):
            for k in range(4):
                by_child[k // 2, 8 * f : 8 * f + 8, 64 * (k % 2) : 64 * (k % 2) + 64] = picked[
                    8 * k : 8 * k + 8, lane_of(f) : lane_of(f) + 64
                ]
        total = jnp.zeros((8, 256), F32)
        for k in range(8):
            lhs = tiles(by_child, pl.ds(k, 8, stride=8))
            total = total + couple(lhs, pairs, step, k)
        outs.append(total)
        if step == 2:
            break
        m = n * n // 4
        if step == 1:
            r = lax.broadcasted_iota(jnp.int32, (n * n, 1), 0)
            k, p, q = r // m, (r % m) // (n // 2), r % (n // 2)
            from_row = (2 * p + k // 2) * n + 2 * q + k % 2
            lane = lax.broadcasted_iota(jnp.int32, (n * n, n * n), 1)
            classes = select((lane == from_row).astype(F32).astype(BF16), table)
        for f in range(6):
            for k in range(4):
                side_by[m * f : m * f + m, 64 * k : 64 * k + 64] = classes[
                    m * k : m * k + m, lane_of(f) : lane_of(f) + 64
                ]
        lifted = jnp.dot(
            side_by[0 : 6 * m, :],
            transfer_ref[3 + step, :, 0:64],
            precision=EXACT,
            preferred_element_type=F32,
        )
        for f in range(6):
            grown[0:m, lane_of(f) : lane_of(f) + 64] = lifted[m * f : m * f + m, :]
        table = grown[0:m, :]

    def own_child(x, step):
        bit_x, bit_y = (gx >> step) & 1, (gy >> step) & 1
        rows = [x[:, 64 * k : 64 * k + 64] for k in range(4)]
        low = jnp.where(bit_y == 1, rows[1], rows[0])
        high = jnp.where(bit_y == 1, rows[3], rows[2])
        return jnp.where(bit_x == 1, high, low)

    reached = own_child(outs[2], 2)
    for step in (1, 0):
        reached = own_child(outs[step] + dot_t(reached, transfer_ref[3 + step, :, 0:64], EXACT), step)
    return jnp.concatenate([reached, jnp.zeros((8, 64), F32)], axis=1)


def far_down(reached, o0, o1, o2, transfer_ref, flat, held):
    half = left_half((6, 128))
    flat[...] = jnp.zeros(flat.shape, F32)
    flat[pl.ds(1, 8, stride=8), :] = reached
    for level, out in ((2, o2), (1, o1), (0, o0)):
        n = PARENTS[level]
        value = out[...] + dot_t(flat[0 : 48 * n, :], transfer_ref[level], EXACT)
        for t in range(2):
            held[t, 0 : 48 * n, :] = value[:, 128 * t : 128 * t + 128]
        offset = min(level, 1)
        for i in range(2 * n):
            for q in range(n):
                both = held[i % 2, pl.ds((i // 2) * 48 + 1 + q, 6, stride=8), :]
                at = 48 * i + offset + 2 * q
                flat[pl.ds(at, 6, stride=8), :] = jnp.where(half, both, 0.0)
                flat[pl.ds(at + 1, 6, stride=8), :] = jnp.where(half, 0.0, both)


def image_rows(i, flat, basis_ref, near_ref):
    d = flat[48 * i : 48 * i + 48, :]
    high = d.astype(BF16)
    low = (d - high.astype(F32)).astype(BF16)
    basis = jnp.concatenate([basis_ref[...]] * 4, axis=0)
    far = dot(jnp.concatenate([high, low], axis=1), basis)
    return near_ref[48 * i : 48 * i + 48, :] + far


def per_row(totals, slot):
    lane = lax.broadcasted_iota(jnp.int32, (1, 128), 1)
    field = lax.broadcasted_iota(jnp.int32, (48, 1), 0) // 8
    out = jnp.zeros((48, 1), F32)
    for f in range(6):
        out = out + jnp.where(
            field == f, jnp.sum(jnp.where(lane == 6 * slot + f, totals, 0.0)), 0.0
        )
    return out


FAR_SCRATCH = [
    pltpu.VMEM((2, 64, 128), F32),
    pltpu.VMEM((64, 384), F32),
    pltpu.VMEM((384, 256), F32),
    pltpu.VMEM((384, 128), F32),
    pltpu.VMEM((2, 192, 128), F32),
]


def second_source(
    pos_ref, all_ref, x_ref, near_ref, o0, o1, o2, high_ref, low_ref, contrast_ref, occupied_ref, basis_ref,
    transfer_ref, u_ref, *rest,
):
    outs, (by_child, grown, side_by, flat, held, skel) = rest[:7], rest[7:]
    reached = far_above(pos_ref, all_ref, (high_ref, low_ref), transfer_ref, by_child, grown, side_by)
    far_down(reached, o0, o1, o2, transfer_ref, flat, held)
    cross = jnp.zeros((48, 128), F32)
    square = jnp.zeros((48, 128), F32)
    for i in range(8):
        u = image_rows(i, flat, basis_ref, near_ref)
        u_ref[48 * i : 48 * i + 48, :] = u
        cross = cross + lanes_to_one(u * x_ref[48 * i : 48 * i + 48, :])
        square = square + lanes_to_one(u * u)
    spread_skeleton(
        lambda i: u_ref[48 * i : 48 * i + 48, :],
        field_row([cross, square]),
        ((contrast_ref, occupied_ref, basis_ref, transfer_ref), outs),
        skel,
    )


def scales(first_totals, second_totals, count):
    s = per_row(first_totals, 0) / count
    beta = jnp.sqrt(s + EPSILON)
    off_one = EPSILON / (s + EPSILON)
    one = s / (s + EPSILON)
    p = per_row(second_totals, 0) / count / (s + EPSILON)
    q = per_row(second_totals, 1) / count / (s + EPSILON)
    r = q + (off_one - p) * ((off_one - p) * one + 2.0 * p)
    h21 = jnp.sqrt(r + EPSILON)
    h11 = one + p
    return dict(
        beta=beta, h11=h11, h21=h21, lean=off_one - p, one=one,
        f12=off_one * h11 / h21, n2=r / (r + EPSILON), off_two=EPSILON / (r + EPSILON),
    )


def totals_of(all_ref):
    return jnp.sum(all_ref[pl.ds(3, 256, stride=4), :], axis=0, keepdims=True)


def last_sums(
    count, pos_ref, all_ref, before_ref, x_ref, u_ref, near_ref, o0, o1, o2, high_ref, low_ref, basis_ref,
    transfer_ref, v_ref, sums_ref, totals_ref, by_child, grown, side_by, flat, held,
):
    first_totals, second_totals = totals_of(before_ref), totals_of(all_ref)
    totals_ref[0:1, :] = first_totals
    totals_ref[1:2, :] = second_totals
    k = scales(first_totals, second_totals, count)
    over, over_two = 1.0 / k["beta"], 1.0 / k["h21"]
    reached = far_above(pos_ref, all_ref, (high_ref, low_ref), transfer_ref, by_child, grown, side_by)
    far_down(reached, o0, o1, o2, transfer_ref, flat, held)
    sums = [jnp.zeros((48, 128), F32)] * 3
    for i in range(8):
        rows = slice(48 * i, 48 * i + 48)
        first = x_ref[rows, :] * over
        image = u_ref[rows, :] * over
        second = (k["lean"] * first + image) * over_two
        v = (k["lean"] * image + image_rows(i, flat, basis_ref, near_ref) * over) * over_two
        v_ref[rows, :] = v
        sums = [
            s + lanes_to_one(w * v) for s, w in zip(sums, (first, second, v))
        ]
    lane = lax.broadcasted_iota(jnp.int32, (1, 128), 1)
    row = jnp.zeros((1, 128), F32)
    for n, acc in enumerate(sums):
        for f in range(6):
            row = row + jnp.where(lane == 16 * n + f, jnp.sum(acc[8 * f : 8 * f + 8, :]), 0.0)
    sums_ref[...] = jnp.broadcast_to(row[None], sums_ref.shape)


def finish(count, sums_ref, totals_ref, x_ref, u_ref, v_ref, third_ref, hess_ref, table):
    k = scales(totals_ref[0:1, :], totals_ref[1:2, :], count)
    total = jnp.sum(sums_ref[...], axis=0, keepdims=True) / count
    lane = lax.broadcasted_iota(jnp.int32, (1, 128), 1)
    field = lax.broadcasted_iota(jnp.int32, (48, 1), 0) // 8

    def rows_of(n):
        out = jnp.zeros((48, 1), F32)
        for f in range(6):
            out = out + jnp.where(
                field == f, jnp.sum(jnp.where(lane == 16 * n + f, total, 0.0)), 0.0
            )
        return out

    c1, c2, t = rows_of(0), rows_of(1), rows_of(2)
    h12, h22 = k["f12"] + c1, k["n2"] + c2
    g = k["off_two"] - c2
    rest = (
        t + g * g * k["n2"] + h12 * h12 * k["one"] + 2.0 * g * c2
        - 2.0 * h12 * c1 - 2.0 * g * h12 * k["f12"]
    )
    h32 = jnp.sqrt(rest + EPSILON)
    over, over_two, over_three = 1.0 / k["beta"], 1.0 / k["h21"], 1.0 / h32
    for i in range(8):
        rows = slice(48 * i, 48 * i + 48)
        first = x_ref[rows, :] * over
        second = (k["lean"] * first + u_ref[rows, :] * over) * over_two
        third_ref[rows, :] = (v_ref[rows, :] + g * second - h12 * first) * over_three
    lane48 = lax.broadcasted_iota(jnp.int32, (48, 128), 1)
    out = jnp.zeros((48, 128), F32)
    for n, h in enumerate((k["beta"], k["h11"], k["h21"], h12, h22, h32)):
        out = out + jnp.where(lane48 == n, h, 0.0)
    table[...] = out
    hess_ref[...] = table[pl.ds(0, 6, stride=8), :][:, 0:6]


def turn(n, s):
    return [(i, (i + s) % n) for i in range(n)]


def to_everyone(blocks):
    return lax.all_to_all(blocks, CLASS_ORDER, 0, 0, tiled=True)


def body(rhs, contrast, occupied, near, basis, transfer, coupling):
    side, _, fields, comps, voxels = rhs.shape
    count = float(128 * 128 * comps * voxels)
    x = rhs.transpose(0, 2, 1, 3, 4).reshape(384, 768)
    contrast = contrast.reshape(64, voxels)
    stacked = transfer.reshape(5, 256, 64)
    stacked = jnp.concatenate([stacked] * 2, axis=2)
    basis = basis.T
    pos = jnp.stack([lax.axis_index(GX), lax.axis_index(GY)]).astype(jnp.int32)
    shape = jax.ShapeDtypeStruct
    inner, *outer = call(
        pair_blocks, [shape((3, 4, 256, 256), BF16)] * 3, [VMEM], [], 10**8, coupling
    )

    def exchange(outs, inner):
        src, up, down, pay, a0, a1, a2 = outs
        src, inner = lax.optimization_barrier((src, inner))
        above = lax.ppermute(up, GX, turn(16, 1))
        below = lax.ppermute(down, GX, turn(16, -1))
        to_left, to_right = call(
            columns, [shape((80, 1024), BF16)] * 2, [SMEM] + [VMEM] * 6,
            [pltpu.VMEM((12, 48, 128), F32)] * 2, 10**6,
            pos, src, a0, a1, a2, above, below,
        )
        pay, to_left, to_right = lax.optimization_barrier((pay, to_left, to_right))
        right = lax.ppermute(to_left, GY, turn(16, -1))
        left = lax.ppermute(to_right, GY, turn(16, 1))
        everyone = to_everyone(pay).reshape(1024, 128)
        parts = call(
            near_and_low,
            [shape((384, 768), F32), shape((192, 256), F32), shape((96, 256), F32), shape((48, 256), F32)],
            [SMEM] + [VMEM] * 10,
            [
                pltpu.VMEM((6, 480, 128), F32), pltpu.VMEM((6, 480, 128), F32), pltpu.VMEM((80, 768), F32),
                pltpu.VMEM((480, 768), BF16), pltpu.VMEM((2, 288, 128), F32), pltpu.VMEM((2, 192, 128), F32),
                pltpu.VMEM((2, 144, 128), F32), pltpu.VMEM((288, 256), F32),
            ],
            10**10,
            pos, src, a0, a1, a2, above, below, left, right, near, inner,
        )
        return everyone, parts

    outs = call(
        first_source, SOURCE_OUTS, [VMEM] * 5, SOURCE_SCRATCH, 10**8,
        x, contrast, occupied, basis, stacked,
    )
    all_one, parts = exchange(outs, inner)
    u, *outs = call(
        second_source, [shape((384, 768), F32)] + SOURCE_OUTS, [SMEM] + [VMEM] * 12,
        FAR_SCRATCH + SOURCE_SCRATCH, 10**8,
        pos, all_one, x, *parts, *outer, contrast, occupied, basis, stacked,
    )
    all_two, parts = exchange(outs, inner)
    v, sums, totals = call(
        functools.partial(last_sums, count),
        [shape((384, 768), F32), shape((256, 1, 128), F32), shape((8, 128), F32)],
        [SMEM] + [VMEM] * 12, FAR_SCRATCH, 10**8,
        pos, all_two, all_one, x, u, *parts, *outer, basis, stacked,
    )
    third, hess = call(
        functools.partial(finish, count),
        [shape((384, 768), F32), shape((6, 6), F32)], [VMEM] * 5, [pltpu.VMEM((48, 128), F32)], 10**6,
        to_everyone(sums).reshape(256, 128), totals, x, u, v,
    )
    third = third.reshape(side, fields, side, comps, voxels).transpose(0, 2, 1, 3, 4)
    return third, hess


def solution(mesh):
    grid = Mesh(mesh.devices.reshape(8, 2, 4, 2, 2), EVERYONE)
    placed = (P(GX, GY, None, None, None), P(GX, GY, None), P(GX, GY), P(), P(), P(), P())
    return jax.shard_map(
        body, mesh=grid, in_specs=placed,
        out_specs=(P(GX, GY, None, None, None), P()), check_vma=False,
    )
```

```python
import functools

import jax
import jax.numpy as jnp
from jax import lax
from jax.experimental import pallas as pl
from jax.experimental.pallas import tpu as pltpu
from jax.sharding import Mesh
from jax.sharding import PartitionSpec as P

F32, BF16 = jnp.float32, jnp.bfloat16
GX = ("z", "c")
GY = ("y", "x1", "x0")
CLASS_ORDER = ("c", "x0", "z", "y", "x1")
EVERYONE = ("z", "c", "y", "x1", "x0")
EPSILON = 1e-06
EXACT = lax.Precision.HIGHEST
HALF = ((1, -1), (1, 0), (1, 1), (0, 1))
AROUND = HALF + tuple((-a, -b) for a, b in HALF)
NEAR_SLOT = {(0, 0): 0, (1, -1): 1, (1, 0): 2, (1, 1): 3, (0, 1): 4}
FAR = [
    (dx, dy)
    for dx in range(-3, 4)
    for dy in range(-3, 4)
    if max(abs(dx), abs(dy)) >= 2 and (dx > 0 or (dx == 0 and dy > 0))
]
VMEM = pl.BlockSpec(memory_space=pltpu.VMEM)
SMEM = pl.BlockSpec(memory_space=pltpu.SMEM)
CHILDREN = [(c, e) for c in range(2) for e in range(2)]
PARENTS = (4, 2, 1)


def dot(a, b):
    return jnp.dot(a, b, preferred_element_type=F32)


def dot_t(a, b, precision=None):
    return lax.dot_general(
        a, b, (((1,), (1,)), ((), ())), preferred_element_type=F32, precision=precision
    )


def call(kernel, outs, specs, scratch, flops, *args):
    moved = sum(a.size * a.dtype.itemsize for a in args)
    return pl.pallas_call(
        kernel,
        out_shape=outs,
        in_specs=specs,
        out_specs=jax.tree.map(lambda _: VMEM, outs),
        scratch_shapes=scratch,
        compiler_params=pltpu.CompilerParams(vmem_limit_bytes=50 * 2**20),
        cost_estimate=pl.CostEstimate(flops=flops, bytes_accessed=moved, transcendentals=0),
    )(*args)


def pair_blocks(first, coupling_ref, *out_refs):
    zero = jnp.zeros((64, 64), F32)
    for level in range(3):
        flipped = {}
        for n, (dp, dq) in enumerate(HALF):
            for c_in, e_in in CHILDREN:
                for c in range(2):
                    row = []
                    for e in range(2):
                        d = (2 * dp + c_in - c, 2 * dq + e_in - e)
                        if max(abs(d[0]), abs(d[1])) < 2:
                            row.append(zero)
                        elif d in FAR:
                            row.append(coupling_ref[first + level, FAR.index(d)])
                        else:
                            k = FAR.index((-d[0], -d[1]))
                            if k not in flipped:
                                flipped[k] = coupling_ref[first + level, k].T
                            row.append(flipped[k])
                    r0 = (2 * c_in + e_in) * 64
                    rows, lanes = slice(r0, r0 + 64), slice(c * 128, c * 128 + 128)
                    block = jnp.concatenate(row, axis=1)
                    high = block.astype(BF16)
                    out_refs[0][level, n, rows, lanes] = high
                    if len(out_refs) > 1:
                        out_refs[1][level, n, rows, lanes] = (block - high.astype(F32)).astype(BF16)


def in_two(x):
    high = x.astype(BF16)
    return high, (x - high.astype(F32)).astype(BF16)


def couple(x, pairs, level, k):
    high, low = in_two(x)
    product = dot if k < 4 else dot_t
    both = product(jnp.concatenate([high, low], axis=0), pairs[0][level, k % 4])
    out = both[0 : x.shape[0]] + both[x.shape[0] :]
    if len(pairs) > 1:
        out = out + product(high, pairs[1][level, k % 4])
    return out


def weight_rows(contrast_ref, occupied_ref, i):
    square = (8, 8)
    here = jnp.broadcast_to(occupied_ref[i : i + 1, :].astype(F32), square)
    same = lax.broadcasted_iota(jnp.int32, square, 0) == lax.broadcasted_iota(jnp.int32, square, 1)
    occupied = jnp.sum(jnp.where(same, here, 0.0), axis=1, keepdims=True)
    w = occupied * contrast_ref[8 * i : 8 * i + 8, :]
    return jnp.concatenate([jnp.concatenate([w] * 6, axis=0)] * 3, axis=1)


def lanes_to_one(x):
    total = x[:, 0:128]
    for k in range(1, x.shape[1] // 128):
        total = total + x[:, 128 * k : 128 * k + 128]
    return total


def field_row(sums):
    lane = lax.broadcasted_iota(jnp.int32, (1, 128), 1)
    row = jnp.zeros((1, 128), F32)
    for n, acc in enumerate(sums):
        for f in range(6):
            row = row + jnp.where(lane == 6 * n + f, jnp.sum(acc[8 * f : 8 * f + 8, :]), 0.0)
    return row


def left_half(shape):
    return lax.broadcasted_iota(jnp.int32, shape, len(shape) - 1) < 64


def tiles(ref, rows):
    return jnp.concatenate([ref[t, rows, :] for t in range(ref.shape[0])], axis=1)


def doubled(x):
    return jnp.concatenate([x, x], axis=1)


def levels_of(ref):
    return [ref.at[:, 0:288, :], ref.at[:, 288:480, :], ref.at[:, 480:624, :]]


def inner_parts(ref):
    return [ref.at[0:192, :], ref.at[192:288, :], ref.at[288:336, :]]


def spread_skeleton(field_at, sums_row, refs, skel):
    contrast_ref, occupied_ref, basis_ref, transfer_ref = refs[0]
    src_ref, up_ref, down_ref, pay_ref, tree_ref = refs[1]
    tree = levels_of(tree_ref)
    twice = jnp.concatenate([basis_ref[...]] * 2, axis=0)
    for i in range(8):
        rows = slice(48 * i, 48 * i + 48)
        s = (weight_rows(contrast_ref, occupied_ref, i) * field_at(i)).astype(BF16)
        for t in range(6):
            src_ref[t, rows, :] = s[:, 128 * t : 128 * t + 128].astype(F32)
        skel[rows, :] = dot_t(s, twice)
        if i == 0:
            down_ref[:, 0:768] = s
        if i == 7:
            up_ref[:, 0:768] = s
    half = left_half((6, 128))
    for level, n in enumerate(PARENTS):
        node = tree[level]
        node[...] = jnp.zeros(node.shape, F32)
        offset = min(level, 1)
        for i in range(2 * n):
            for q in range(n):
                at = 48 * i + offset + 2 * q
                node[i % 2, pl.ds((i // 2 + 1) * 48 + 1 + q, 6, stride=8), :] = jnp.where(
                    half, skel[pl.ds(at, 6, stride=8), :], skel[pl.ds(at + 1, 6, stride=8), :]
                )
        lanes = slice(768 + 256 * level, 1024 + 256 * level)
        up_ref[:, lanes] = tiles(node, slice(48 * n, 48 * n + 48)).astype(BF16)
        down_ref[:, lanes] = tiles(node, slice(48, 96)).astype(BF16)
        skel[0 : 48 * n, :] = jnp.dot(
            tiles(node, slice(48, 48 * n + 48)),
            doubled(transfer_ref[level]),
            precision=EXACT,
            preferred_element_type=F32,
        )
    top = skel[pl.ds(1, 6, stride=8), :]
    pay = jnp.concatenate([jnp.where(half[0:3], top[0:3, :], top[3:6, :]), sums_row], axis=0)
    pay_ref[...] = jnp.broadcast_to(pay[None], pay_ref.shape)


SOURCE_OUTS = [
    jax.ShapeDtypeStruct((6, 384, 128), F32),
    jax.ShapeDtypeStruct((48, 1536), BF16),
    jax.ShapeDtypeStruct((48, 1536), BF16),
    jax.ShapeDtypeStruct((256, 4, 128), F32),
    jax.ShapeDtypeStruct((2, 624, 128), F32),
]
SOURCE_SCRATCH = [pltpu.VMEM((384, 128), F32)]


def first_source(x_ref, contrast_ref, occupied_ref, basis_ref, transfer_ref, *rest):
    outs, skel = rest[:5], rest[5]
    acc = jnp.zeros((48, 128), F32)
    for i in range(8):
        x = x_ref[48 * i : 48 * i + 48, :]
        acc = acc + lanes_to_one(x * x)
    spread_skeleton(
        lambda i: x_ref[48 * i : 48 * i + 48, :],
        field_row([acc]),
        ((contrast_ref, occupied_ref, basis_ref, transfer_ref), outs),
        skel,
    )


def columns(pos_ref, src_ref, tree_ref, above_ref, below_ref, left_ref, right_ref, above, below):
    gx = pos_ref[0]
    for t in range(12):
        lanes = slice(128 * t, 128 * t + 128)
        above[t] = above_ref[:, lanes].astype(F32) * (gx > 0).astype(F32)
        below[t] = below_ref[:, lanes].astype(F32) * (gx < 15).astype(F32)
    for out, side in ((left_ref, 0), (right_ref, 1)):
        j = 7 * side
        for t in range(6):
            out[0:60, 128 * t : 128 * t + 128] = jnp.concatenate(
                [
                    above[t, pl.ds(j, 6, stride=8), :],
                    src_ref[t, pl.ds(j, 48, stride=8), :],
                    below[t, pl.ds(j, 6, stride=8), :],
                ],
                axis=0,
            ).astype(BF16)
            out[60:80, 128 * t : 128 * t + 128] = jnp.zeros((20, 128), BF16)
        for t in range(2):
            parts = []
            for level, (node, n) in enumerate(zip(levels_of(tree_ref), PARENTS)):
                q = n if side else 1
                parts += [
                    above[6 + 2 * level + t, pl.ds(q, 6, stride=8), :],
                    node[t, pl.ds(48 + q, 6 * n, stride=8), :],
                    below[6 + 2 * level + t, pl.ds(q, 6, stride=8), :],
                ]
            parts.append(jnp.zeros((2, 128), F32))
            out[:, 768 + 128 * t : 896 + 128 * t] = jnp.concatenate(parts, axis=0).astype(BF16)


def near_and_low(
    pos_ref, src_ref, tree_ref, above_ref, below_ref, left_ref, right_ref, near_ref, inner_ref,
    near_out, inner_out, wide, moved, edge, placed, n0, n1, n2, turned,
):
    gx, gy = pos_ref[0], pos_ref[1]
    up = (gx > 0).astype(F32)
    down = (gx < 15).astype(F32)
    for t in range(6):
        lanes = slice(128 * t, 128 * t + 128)
        wide[t, 0:48, :] = above_ref[:, lanes].astype(F32) * up
        wide[t, 48:432, :] = src_ref[t]
        wide[t, 432:480, :] = below_ref[:, lanes].astype(F32) * down
    flags = ((gy > 0).astype(F32), (gy < 15).astype(F32))
    first = True
    for b in (0, -1, 1):
        side_ref, flag = ((left_ref, flags[0]), (right_ref, flags[1]))[b > 0]
        if b != 0:
            edge[...] = side_ref[:, 0:768].astype(F32) * flag
        for t in range(6):
            lanes = slice(128 * t, 128 * t + 128)
            if b == 0:
                placed[:, lanes] = wide[t].astype(BF16)
                continue
            if b < 0:
                moved[t, 1:480, :] = wide[t, 0:479, :]
                moved[t, pl.ds(0, 60, stride=8), :] = edge[0:60, lanes]
            else:
                moved[t, 0:479, :] = wide[t, 1:480, :]
                moved[t, pl.ds(7, 60, stride=8), :] = edge[0:60, lanes]
            placed[:, lanes] = moved[t].astype(BF16)
        for a in (-1, 0, 1):
            lhs = placed[48 * (1 + a) : 48 * (1 + a) + 384, :]
            if (a, b) in NEAR_SLOT:
                part = dot(lhs, near_ref[NEAR_SLOT[a, b]])
            else:
                part = dot_t(lhs, near_ref[NEAR_SLOT[-a, -b]])
            if first:
                near_out[...] = part
                first = False
            else:
                near_out[...] += part
    start = 0
    for level, (node, full, out, n) in enumerate(
        zip(levels_of(tree_ref), (n0, n1, n2), inner_parts(inner_out), PARENTS)
    ):
        size, lanes = 48 * (n + 2), slice(768 + 256 * level, 1024 + 256 * level)
        for t in range(2):
            lane = slice(lanes.start + 128 * t, lanes.start + 128 * t + 128)
            full[t] = node[t]
            full[t, 0:48, :] = above_ref[:, lane].astype(F32) * up
            full[t, size - 48 : size, :] = below_ref[:, lane].astype(F32) * down
        for side_ref, flag, q in ((left_ref, flags[0], 0), (right_ref, flags[1], n + 1)):
            edge[:, 0:256] = side_ref[:, 768:1024].astype(F32) * flag
            for t in range(2):
                full[t, pl.ds(q, 6 * (n + 2), stride=8), :] = edge[
                    start : start + 6 * (n + 2), 128 * t : 128 * t + 128
                ]
        total = jnp.zeros((48 * n, 256), F32)
        for dq in (-1, 0, 1):
            for t in range(2):
                lane = slice(128 * t, 128 * t + 128)
                if dq == 0:
                    turned[0:size, lane] = full[t]
                elif dq < 0:
                    turned[1:size, lane] = full[t, 0 : size - 1, :]
                    turned[0:1, lane] = full[t, 0:1, :]
                else:
                    turned[0 : size - 1, lane] = full[t, 1:size, :]
                    turned[size - 1 : size, lane] = full[t, 0:1, :]
            for k, (dp, dq_k) in enumerate(AROUND):
                if dq_k == dq:
                    lhs = turned[48 * (1 + dp) : 48 * (1 + dp) + 48 * n, :]
                    total = total + couple(lhs, (inner_ref,), level, k)
        out[...] = total
        start += 6 * (n + 2)


def lane_of(f):
    return (f % 3) * 128 + (f // 3) * 64


def select(chosen, table):
    high, low = in_two(table)
    return dot(chosen, high) + dot(chosen, low)


def far_above(pos_ref, all_ref, pairs, transfer_ref, by_child, grown, side_by):
    gx, gy = pos_ref[0], pos_ref[1]
    table = jnp.concatenate([all_ref[pl.ds(m, 256, stride=4), :] for m in range(3)], axis=1)
    classes = table
    row = lax.broadcasted_iota(jnp.int32, (32, 1), 0)
    around, child = row % 8, row // 8
    shift_p = sum(jnp.where(around == k, dp, 0) for k, (dp, _) in enumerate(AROUND))
    shift_q = sum(jnp.where(around == k, dq, 0) for k, (_, dq) in enumerate(AROUND))
    outs = []
    for step in range(3):
        n = 16 >> step
        at_p, at_q = (gx >> (step + 1)) + shift_p, (gy >> (step + 1)) + shift_q
        inside = (at_p >= 0) & (at_p < n // 2) & (at_q >= 0) & (at_q < n // 2)
        if step == 0:
            where = child * (n * n // 4) + at_p * (n // 2) + at_q
        else:
            where = (2 * at_p + child // 2) * n + 2 * at_q + child % 2
        lane = lax.broadcasted_iota(jnp.int32, (32, n * n), 1)
        chosen = ((lane == where) & inside).astype(F32).astype(BF16)
        picked = select(chosen, table)
        by_child[...] = jnp.zeros(by_child.shape, F32)
        for f in range(6):
            for k in range(4):
                by_child[k // 2, 8 * f : 8 * f + 8, 64 * (k % 2) : 64 * (k % 2) + 64] = picked[
                    8 * k : 8 * k + 8, lane_of(f) : lane_of(f) + 64
                ]
        total = jnp.zeros((8, 256), F32)
        for k in range(8):
            lhs = tiles(by_child, pl.ds(k, 8, stride=8))
            total = total + couple(lhs, pairs, step, k)
        outs.append(total)
        if step == 2:
            break
        m = n * n // 4
        if step == 1:
            r = lax.broadcasted_iota(jnp.int32, (n * n, 1), 0)
            k, p, q = r // m, (r % m) // (n // 2), r % (n // 2)
            from_row = (2 * p + k // 2) * n + 2 * q + k % 2
            lane = lax.broadcasted_iota(jnp.int32, (n * n, n * n), 1)
            classes = select((lane == from_row).astype(F32).astype(BF16), table)
        for f in range(6):
            for k in range(4):
                side_by[m * f : m * f + m, 64 * k : 64 * k + 64] = classes[
                    m * k : m * k + m, lane_of(f) : lane_of(f) + 64
                ]
        lifted = jnp.dot(
            side_by[0 : 6 * m, :],
            transfer_ref[3 + step],
            precision=EXACT,
            preferred_element_type=F32,
        )
        for f in range(6):
            grown[0:m, lane_of(f) : lane_of(f) + 64] = lifted[m * f : m * f + m, :]
        table = grown[0:m, :]

    def own_child(x, step):
        bit_x, bit_y = (gx >> step) & 1, (gy >> step) & 1
        rows = [x[:, 64 * k : 64 * k + 64] for k in range(4)]
        low = jnp.where(bit_y == 1, rows[1], rows[0])
        high = jnp.where(bit_y == 1, rows[3], rows[2])
        return jnp.where(bit_x == 1, high, low)

    reached = own_child(outs[2], 2)
    for step in (1, 0):
        reached = own_child(outs[step] + dot_t(reached, transfer_ref[3 + step], EXACT), step)
    return jnp.concatenate([reached, jnp.zeros((8, 64), F32)], axis=1)


def far_down(reached, inner_ref, transfer_ref, flat, held):
    o0, o1, o2 = inner_parts(inner_ref)
    half = left_half((6, 128))
    flat[...] = jnp.zeros(flat.shape, F32)
    flat[pl.ds(1, 8, stride=8), :] = reached
    for level, out in ((2, o2), (1, o1), (0, o0)):
        n = PARENTS[level]
        value = out[...] + dot_t(flat[0 : 48 * n, :], doubled(transfer_ref[level]), EXACT)
        for t in range(2):
            held[t, 0 : 48 * n, :] = value[:, 128 * t : 128 * t + 128]
        offset = min(level, 1)
        for i in range(2 * n):
            for q in range(n):
                both = held[i % 2, pl.ds((i // 2) * 48 + 1 + q, 6, stride=8), :]
                at = 48 * i + offset + 2 * q
                flat[pl.ds(at, 6, stride=8), :] = jnp.where(half, both, 0.0)
                flat[pl.ds(at + 1, 6, stride=8), :] = jnp.where(half, 0.0, both)


def image_rows(i, flat, basis_ref, near_ref):
    d = flat[48 * i : 48 * i + 48, :]
    high = d.astype(BF16)
    low = (d - high.astype(F32)).astype(BF16)
    basis = jnp.concatenate([basis_ref[...]] * 4, axis=0)
    far = dot(jnp.concatenate([high, low], axis=1), basis)
    return near_ref[48 * i : 48 * i + 48, :] + far


def per_row(totals, slot):
    lane = lax.broadcasted_iota(jnp.int32, (1, 128), 1)
    field = lax.broadcasted_iota(jnp.int32, (48, 1), 0) // 8
    out = jnp.zeros((48, 1), F32)
    for f in range(6):
        out = out + jnp.where(
            field == f, jnp.sum(jnp.where(lane == 6 * slot + f, totals, 0.0)), 0.0
        )
    return out


FAR_SCRATCH = [
    pltpu.VMEM((2, 64, 128), F32),
    pltpu.VMEM((64, 384), F32),
    pltpu.VMEM((384, 256), F32),
    pltpu.VMEM((384, 128), F32),
    pltpu.VMEM((2, 192, 128), F32),
]


def second_source(
    pos_ref, all_ref, x_ref, near_ref, inner_ref, high_ref, low_ref, contrast_ref, occupied_ref, basis_ref,
    transfer_ref, u_ref, *rest,
):
    outs, (by_child, grown, side_by, flat, held, skel) = rest[:5], rest[5:]
    reached = far_above(pos_ref, all_ref, (high_ref, low_ref), transfer_ref, by_child, grown, side_by)
    far_down(reached, inner_ref, transfer_ref, flat, held)
    cross = jnp.zeros((48, 128), F32)
    square = jnp.zeros((48, 128), F32)
    for i in range(8):
        u = image_rows(i, flat, basis_ref, near_ref)
        u_ref[48 * i : 48 * i + 48, :] = u
        cross = cross + lanes_to_one(u * x_ref[48 * i : 48 * i + 48, :])
        square = square + lanes_to_one(u * u)
    spread_skeleton(
        lambda i: u_ref[48 * i : 48 * i + 48, :],
        field_row([cross, square]),
        ((contrast_ref, occupied_ref, basis_ref, transfer_ref), outs),
        skel,
    )


def scales(first_totals, second_totals, count):
    s = per_row(first_totals, 0) / count
    beta = jnp.sqrt(s + EPSILON)
    off_one = EPSILON / (s + EPSILON)
    one = s / (s + EPSILON)
    p = per_row(second_totals, 0) / count / (s + EPSILON)
    q = per_row(second_totals, 1) / count / (s + EPSILON)
    r = q + (off_one - p) * ((off_one - p) * one + 2.0 * p)
    h21 = jnp.sqrt(r + EPSILON)
    h11 = one + p
    return dict(
        beta=beta, h11=h11, h21=h21, lean=off_one - p, one=one,
        f12=off_one * h11 / h21, n2=r / (r + EPSILON), off_two=EPSILON / (r + EPSILON),
    )


def totals_of(all_ref):
    return jnp.sum(all_ref[pl.ds(3, 256, stride=4), :], axis=0, keepdims=True)


def last_sums(
    count, pos_ref, all_ref, before_ref, x_ref, u_ref, near_ref, inner_ref, high_ref, low_ref, basis_ref,
    transfer_ref, v_ref, sums_ref, totals_ref, by_child, grown, side_by, flat, held,
):
    first_totals, second_totals = totals_of(before_ref), totals_of(all_ref)
    totals_ref[0:1, :] = first_totals
    totals_ref[1:2, :] = second_totals
    k = scales(first_totals, second_totals, count)
    over, over_two = 1.0 / k["beta"], 1.0 / k["h21"]
    reached = far_above(pos_ref, all_ref, (high_ref, low_ref), transfer_ref, by_child, grown, side_by)
    far_down(reached, inner_ref, transfer_ref, flat, held)
    sums = [jnp.zeros((48, 128), F32)] * 3
    for i in range(8):
        rows = slice(48 * i, 48 * i + 48)
        first = x_ref[rows, :] * over
        image = u_ref[rows, :] * over
        second = (k["lean"] * first + image) * over_two
        v = (k["lean"] * image + image_rows(i, flat, basis_ref, near_ref) * over) * over_two
        v_ref[rows, :] = v
        sums = [
            s + lanes_to_one(w * v) for s, w in zip(sums, (first, second, v))
        ]
    lane = lax.broadcasted_iota(jnp.int32, (1, 128), 1)
    row = jnp.zeros((1, 128), F32)
    for n, acc in enumerate(sums):
        for f in range(6):
            row = row + jnp.where(lane == 16 * n + f, jnp.sum(acc[8 * f : 8 * f + 8, :]), 0.0)
    sums_ref[...] = jnp.broadcast_to(row[None], sums_ref.shape)


def finish(count, sums_ref, totals_ref, x_ref, u_ref, v_ref, third_ref, hess_ref, table):
    k = scales(totals_ref[0:1, :], totals_ref[1:2, :], count)
    total = jnp.sum(sums_ref[...], axis=0, keepdims=True) / count
    lane = lax.broadcasted_iota(jnp.int32, (1, 128), 1)
    field = lax.broadcasted_iota(jnp.int32, (48, 1), 0) // 8

    def rows_of(n):
        out = jnp.zeros((48, 1), F32)
        for f in range(6):
            out = out + jnp.where(
                field == f, jnp.sum(jnp.where(lane == 16 * n + f, total, 0.0)), 0.0
            )
        return out

    c1, c2, t = rows_of(0), rows_of(1), rows_of(2)
    h12, h22 = k["f12"] + c1, k["n2"] + c2
    g = k["off_two"] - c2
    rest = (
        t + g * g * k["n2"] + h12 * h12 * k["one"] + 2.0 * g * c2
        - 2.0 * h12 * c1 - 2.0 * g * h12 * k["f12"]
    )
    h32 = jnp.sqrt(rest + EPSILON)
    over, over_two, over_three = 1.0 / k["beta"], 1.0 / k["h21"], 1.0 / h32
    for i in range(8):
        rows = slice(48 * i, 48 * i + 48)
        first = x_ref[rows, :] * over
        second = (k["lean"] * first + u_ref[rows, :] * over) * over_two
        third_ref[rows, :] = (v_ref[rows, :] + g * second - h12 * first) * over_three
    lane48 = lax.broadcasted_iota(jnp.int32, (48, 128), 1)
    out = jnp.zeros((48, 128), F32)
    for n, h in enumerate((k["beta"], k["h11"], k["h21"], h12, h22, h32)):
        out = out + jnp.where(lane48 == n, h, 0.0)
    table[...] = out
    hess_ref[...] = table[pl.ds(0, 6, stride=8), :][:, 0:6]


def turn(n, s):
    return [(i, (i + s) % n) for i in range(n)]


def to_everyone(blocks):
    return lax.all_to_all(blocks, CLASS_ORDER, 0, 0, tiled=True)


def body(rhs, contrast, occupied, near, basis, transfer, coupling):
    side, _, fields, comps, voxels = rhs.shape
    count = float(128 * 128 * comps * voxels)
    x = rhs.transpose(0, 2, 1, 3, 4).reshape(384, 768)
    contrast = contrast.reshape(64, voxels)
    stacked = transfer.reshape(5, 256, 64)
    basis = basis.T
    pos = jnp.stack([lax.axis_index(GX), lax.axis_index(GY)]).astype(jnp.int32)
    shape = jax.ShapeDtypeStruct
    blocks = shape((3, 4, 256, 256), BF16)
    (inner,) = call(
        functools.partial(pair_blocks, 0), [blocks], [VMEM], [], 10**8, coupling
    )
    outer = call(
        functools.partial(pair_blocks, 3), [blocks] * 2, [VMEM], [], 10**8, coupling
    )

    def exchange(outs, inner):
        src, up, down, pay, tree = outs
        src, inner = lax.optimization_barrier((src, inner))
        above = lax.ppermute(up, GX, turn(16, 1))
        below = lax.ppermute(down, GX, turn(16, -1))
        to_left, to_right = call(
            columns, [shape((80, 1024), BF16)] * 2, [SMEM] + [VMEM] * 4,
            [pltpu.VMEM((12, 48, 128), F32)] * 2, 10**6,
            pos, src, tree, above, below,
        )
        pay, to_left, to_right = lax.optimization_barrier((pay, to_left, to_right))
        right = lax.ppermute(to_left, GY, turn(16, -1))
        left = lax.ppermute(to_right, GY, turn(16, 1))
        everyone = to_everyone(pay).reshape(1024, 128)
        parts = call(
            near_and_low,
            [shape((384, 768), F32), shape((336, 256), F32)],
            [SMEM] + [VMEM] * 8,
            [
                pltpu.VMEM((6, 480, 128), F32), pltpu.VMEM((6, 480, 128), F32), pltpu.VMEM((80, 768), F32),
                pltpu.VMEM((480, 768), BF16), pltpu.VMEM((2, 288, 128), F32), pltpu.VMEM((2, 192, 128), F32),
                pltpu.VMEM((2, 144, 128), F32), pltpu.VMEM((288, 256), F32),
            ],
            10**10,
            pos, src, tree, above, below, left, right, near, inner,
        )
        return everyone, parts

    outs = call(
        first_source, SOURCE_OUTS, [VMEM] * 5, SOURCE_SCRATCH, 10**8,
        x, contrast, occupied, basis, stacked,
    )
    all_one, parts = exchange(outs, inner)
    u, *outs = call(
        second_source, [shape((384, 768), F32)] + SOURCE_OUTS, [SMEM] + [VMEM] * 10,
        FAR_SCRATCH + SOURCE_SCRATCH, 10**8,
        pos, all_one, x, *parts, *outer, contrast, occupied, basis, stacked,
    )
    all_two, parts = exchange(outs, inner)
    v, sums, totals = call(
        functools.partial(last_sums, count),
        [shape((384, 768), F32), shape((256, 1, 128), F32), shape((8, 128), F32)],
        [SMEM] + [VMEM] * 10, FAR_SCRATCH, 10**8,
        pos, all_two, all_one, x, u, *parts, *outer, basis, stacked,
    )
    third, hess = call(
        functools.partial(finish, count),
        [shape((384, 768), F32), shape((6, 6), F32)], [VMEM] * 5, [pltpu.VMEM((48, 128), F32)], 10**6,
        to_everyone(sums).reshape(256, 128), totals, x, u, v,
    )
    third = third.reshape(side, fields, side, comps, voxels).transpose(0, 2, 1, 3, 4)
    return third, hess


def solution(mesh):
    grid = Mesh(mesh.devices.reshape(8, 2, 4, 2, 2), EVERYONE)
    placed = (P(GX, GY, None, None, None), P(GX, GY, None), P(GX, GY), P(), P(), P(), P())
    return jax.shard_map(
        body, mesh=grid, in_specs=placed,
        out_specs=(P(GX, GY, None, None, None), P()), check_vma=False,
    )
```

```python
import functools

import jax
import jax.numpy as jnp
from jax import lax
from jax.experimental import pallas as pl
from jax.experimental.pallas import tpu as pltpu
from jax.sharding import Mesh
from jax.sharding import PartitionSpec as P

F32, BF16 = jnp.float32, jnp.bfloat16
GX = ("z", "c")
GY = ("y", "x1", "x0")
CLASS_ORDER = ("c", "x0", "z", "y", "x1")
EVERYONE = ("z", "c", "y", "x1", "x0")
EPSILON = 1e-06
EXACT = lax.Precision.HIGHEST
HALF = ((1, -1), (1, 0), (1, 1), (0, 1))
AROUND = HALF + tuple((-a, -b) for a, b in HALF)
NEAR_SLOT = {(0, 0): 0, (1, -1): 1, (1, 0): 2, (1, 1): 3, (0, 1): 4}
FAR = [
    (dx, dy)
    for dx in range(-3, 4)
    for dy in range(-3, 4)
    if max(abs(dx), abs(dy)) >= 2 and (dx > 0 or (dx == 0 and dy > 0))
]
VMEM = pl.BlockSpec(memory_space=pltpu.VMEM)
SMEM = pl.BlockSpec(memory_space=pltpu.SMEM)
CHILDREN = [(c, e) for c in range(2) for e in range(2)]
PARENTS = (4, 2, 1)


def dot(a, b):
    return jnp.dot(a, b, preferred_element_type=F32)


def dot_t(a, b, precision=None):
    return lax.dot_general(
        a, b, (((1,), (1,)), ((), ())), preferred_element_type=F32, precision=precision
    )


def call(kernel, outs, specs, scratch, flops, *args):
    moved = sum(a.size * a.dtype.itemsize for a in args)
    return pl.pallas_call(
        kernel,
        out_shape=outs,
        in_specs=specs,
        out_specs=jax.tree.map(lambda _: VMEM, outs),
        scratch_shapes=scratch,
        compiler_params=pltpu.CompilerParams(vmem_limit_bytes=50 * 2**20),
        cost_estimate=pl.CostEstimate(flops=flops, bytes_accessed=moved, transcendentals=0),
    )(*args)


def pair_blocks(first, coupling_ref, *out_refs):
    zero = jnp.zeros((64, 64), F32)
    for level in range(3):
        flipped = {}
        for n, (dp, dq) in enumerate(HALF):
            for c_in, e_in in CHILDREN:
                for c in range(2):
                    row = []
                    for e in range(2):
                        d = (2 * dp + c_in - c, 2 * dq + e_in - e)
                        if max(abs(d[0]), abs(d[1])) < 2:
                            row.append(zero)
                        elif d in FAR:
                            row.append(coupling_ref[first + level, FAR.index(d)])
                        else:
                            k = FAR.index((-d[0], -d[1]))
                            if k not in flipped:
                                flipped[k] = coupling_ref[first + level, k].T
                            row.append(flipped[k])
                    r0 = (2 * c_in + e_in) * 64
                    rows, lanes = slice(r0, r0 + 64), slice(c * 128, c * 128 + 128)
                    block = jnp.concatenate(row, axis=1)
                    high = block.astype(BF16)
                    out_refs[0][level, n, rows, lanes] = high
                    if len(out_refs) > 1:
                        out_refs[1][level, n, rows, lanes] = (block - high.astype(F32)).astype(BF16)


def in_two(x):
    high = x.astype(BF16)
    return high, (x - high.astype(F32)).astype(BF16)


def couple(x, pairs, level, k):
    high, low = in_two(x)
    product = dot if k < 4 else dot_t
    both = product(jnp.concatenate([high, low], axis=0), pairs[0][level, k % 4])
    out = both[0 : x.shape[0]] + both[x.shape[0] :]
    if len(pairs) > 1:
        out = out + product(high, pairs[1][level, k % 4])
    return out


def weight_rows(contrast_ref, occupied_ref, i):
    square = (8, 8)
    here = jnp.broadcast_to(occupied_ref[i : i + 1, :].astype(F32), square)
    same = lax.broadcasted_iota(jnp.int32, square, 0) == lax.broadcasted_iota(jnp.int32, square, 1)
    occupied = jnp.sum(jnp.where(same, here, 0.0), axis=1, keepdims=True)
    w = occupied * contrast_ref[8 * i : 8 * i + 8, :]
    return jnp.concatenate([jnp.concatenate([w] * 6, axis=0)] * 3, axis=1)


def lanes_to_one(x):
    total = x[:, 0:128]
    for k in range(1, x.shape[1] // 128):
        total = total + x[:, 128 * k : 128 * k + 128]
    return total


def field_row(sums):
    lane = lax.broadcasted_iota(jnp.int32, (1, 128), 1)
    row = jnp.zeros((1, 128), F32)
    for n, acc in enumerate(sums):
        for f in range(6):
            row = row + jnp.where(lane == 6 * n + f, jnp.sum(acc[8 * f : 8 * f + 8, :]), 0.0)
    return row


def left_half(shape):
    return lax.broadcasted_iota(jnp.int32, shape, len(shape) - 1) < 64


def tiles(ref, rows):
    return jnp.concatenate([ref[t, rows, :] for t in range(ref.shape[0])], axis=1)


def doubled(x):
    return jnp.concatenate([x, x], axis=1)


def levels_of(ref):
    return [ref.at[:, 0:288, :], ref.at[:, 288:480, :], ref.at[:, 480:624, :]]


def inner_parts(ref):
    return [ref.at[0:192, :], ref.at[192:288, :], ref.at[288:336, :]]


def spread_skeleton(field_at, sums_row, refs, skel):
    contrast_ref, occupied_ref, basis_ref, transfer_ref = refs[0]
    src_ref, up_ref, down_ref, pay_ref, tree_ref = refs[1]
    tree = levels_of(tree_ref)
    twice = jnp.concatenate([basis_ref[...]] * 2, axis=0)
    for i in range(8):
        rows = slice(48 * i, 48 * i + 48)
        s = (weight_rows(contrast_ref, occupied_ref, i) * field_at(i)).astype(BF16)
        for t in range(6):
            src_ref[t, rows, :] = s[:, 128 * t : 128 * t + 128].astype(F32)
        skel[rows, :] = dot_t(s, twice)
        if i == 0:
            down_ref[:, 0:768] = s
        if i == 7:
            up_ref[:, 0:768] = s
    half = left_half((6, 128))
    for level, n in enumerate(PARENTS):
        node = tree[level]
        node[...] = jnp.zeros(node.shape, F32)
        offset = min(level, 1)
        for i in range(2 * n):
            for q in range(n):
                at = 48 * i + offset + 2 * q
                node[i % 2, pl.ds((i // 2 + 1) * 48 + 1 + q, 6, stride=8), :] = jnp.where(
                    half, skel[pl.ds(at, 6, stride=8), :], skel[pl.ds(at + 1, 6, stride=8), :]
                )
        lanes = slice(768 + 256 * level, 1024 + 256 * level)
        up_ref[:, lanes] = tiles(node, slice(48 * n, 48 * n + 48)).astype(BF16)
        down_ref[:, lanes] = tiles(node, slice(48, 96)).astype(BF16)
        skel[0 : 48 * n, :] = jnp.dot(
            tiles(node, slice(48, 48 * n + 48)),
            doubled(transfer_ref[level]),
            precision=EXACT,
            preferred_element_type=F32,
        )
    top = skel[pl.ds(1, 6, stride=8), :]
    pay = jnp.concatenate([jnp.where(half[0:3], top[0:3, :], top[3:6, :]), sums_row], axis=0)
    pay_ref[...] = jnp.broadcast_to(pay[None], pay_ref.shape)


SOURCE_OUTS = [
    jax.ShapeDtypeStruct((6, 384, 128), F32),
    jax.ShapeDtypeStruct((48, 1536), BF16),
    jax.ShapeDtypeStruct((48, 1536), BF16),
    jax.ShapeDtypeStruct((256, 4, 128), F32),
    jax.ShapeDtypeStruct((2, 624, 128), F32),
]
SOURCE_SCRATCH = [pltpu.VMEM((384, 128), F32)]


def first_source(x_ref, contrast_ref, occupied_ref, basis_ref, transfer_ref, *rest):
    outs, skel = rest[:5], rest[5]
    acc = jnp.zeros((48, 128), F32)
    for i in range(8):
        x = x_ref[48 * i : 48 * i + 48, :]
        acc = acc + lanes_to_one(x * x)
    spread_skeleton(
        lambda i: x_ref[48 * i : 48 * i + 48, :],
        field_row([acc]),
        ((contrast_ref, occupied_ref, basis_ref, transfer_ref), outs),
        skel,
    )


def columns(pos_ref, src_ref, tree_ref, above_ref, below_ref, left_ref, right_ref, above, below):
    gx = pos_ref[0]
    for t in range(12):
        lanes = slice(128 * t, 128 * t + 128)
        above[t] = above_ref[:, lanes].astype(F32) * (gx > 0).astype(F32)
        below[t] = below_ref[:, lanes].astype(F32) * (gx < 15).astype(F32)
    for out, side in ((left_ref, 0), (right_ref, 1)):
        j = 7 * side
        for t in range(6):
            out[0:60, 128 * t : 128 * t + 128] = jnp.concatenate(
                [
                    above[t, pl.ds(j, 6, stride=8), :],
                    src_ref[t, pl.ds(j, 48, stride=8), :],
                    below[t, pl.ds(j, 6, stride=8), :],
                ],
                axis=0,
            ).astype(BF16)
            out[60:80, 128 * t : 128 * t + 128] = jnp.zeros((20, 128), BF16)
        for t in range(2):
            parts = []
            for level, (node, n) in enumerate(zip(levels_of(tree_ref), PARENTS)):
                q = n if side else 1
                parts += [
                    above[6 + 2 * level + t, pl.ds(q, 6, stride=8), :],
                    node[t, pl.ds(48 + q, 6 * n, stride=8), :],
                    below[6 + 2 * level + t, pl.ds(q, 6, stride=8), :],
                ]
            parts.append(jnp.zeros((2, 128), F32))
            out[:, 768 + 128 * t : 896 + 128 * t] = jnp.concatenate(parts, axis=0).astype(BF16)


def near_and_low(
    pos_ref, src_ref, tree_ref, above_ref, below_ref, left_ref, right_ref, near_hbm, inner_ref,
    near_out, inner_out, near_ref, arrived, wide, moved, edge, placed, n0, n1, n2, turned,
):
    copies = [
        pltpu.make_async_copy(near_hbm.at[n], near_ref.at[n], arrived.at[n]) for n in range(5)
    ]
    for n in (2, 0, 3, 1, 4):
        copies[n].start()
    waited = set()
    gx, gy = pos_ref[0], pos_ref[1]
    up = (gx > 0).astype(F32)
    down = (gx < 15).astype(F32)
    for t in range(6):
        lanes = slice(128 * t, 128 * t + 128)
        wide[t, 0:48, :] = above_ref[:, lanes].astype(F32) * up
        wide[t, 48:432, :] = src_ref[t]
        wide[t, 432:480, :] = below_ref[:, lanes].astype(F32) * down
    flags = ((gy > 0).astype(F32), (gy < 15).astype(F32))
    first = True
    for b in (0, -1, 1):
        side_ref, flag = ((left_ref, flags[0]), (right_ref, flags[1]))[b > 0]
        if b != 0:
            edge[...] = side_ref[:, 0:768].astype(F32) * flag
        for t in range(6):
            lanes = slice(128 * t, 128 * t + 128)
            if b == 0:
                placed[:, lanes] = wide[t].astype(BF16)
                continue
            if b < 0:
                moved[t, 1:480, :] = wide[t, 0:479, :]
                moved[t, pl.ds(0, 60, stride=8), :] = edge[0:60, lanes]
            else:
                moved[t, 0:479, :] = wide[t, 1:480, :]
                moved[t, pl.ds(7, 60, stride=8), :] = edge[0:60, lanes]
            placed[:, lanes] = moved[t].astype(BF16)
        for a in (-1, 0, 1):
            slot = NEAR_SLOT[(a, b) if (a, b) in NEAR_SLOT else (-a, -b)]
            if slot not in waited:
                waited.add(slot)
                copies[slot].wait()
            lhs = placed[48 * (1 + a) : 48 * (1 + a) + 384, :]
            if (a, b) in NEAR_SLOT:
                part = dot(lhs, near_ref[slot])
            else:
                part = dot_t(lhs, near_ref[slot])
            if first:
                near_out[...] = part
                first = False
            else:
                near_out[...] += part
    start = 0
    for level, (node, full, out, n) in enumerate(
        zip(levels_of(tree_ref), (n0, n1, n2), inner_parts(inner_out), PARENTS)
    ):
        size, lanes = 48 * (n + 2), slice(768 + 256 * level, 1024 + 256 * level)
        for t in range(2):
            lane = slice(lanes.start + 128 * t, lanes.start + 128 * t + 128)
            full[t] = node[t]
            full[t, 0:48, :] = above_ref[:, lane].astype(F32) * up
            full[t, size - 48 : size, :] = below_ref[:, lane].astype(F32) * down
        for side_ref, flag, q in ((left_ref, flags[0], 0), (right_ref, flags[1], n + 1)):
            edge[:, 0:256] = side_ref[:, 768:1024].astype(F32) * flag
            for t in range(2):
                full[t, pl.ds(q, 6 * (n + 2), stride=8), :] = edge[
                    start : start + 6 * (n + 2), 128 * t : 128 * t + 128
                ]
        total = jnp.zeros((48 * n, 256), F32)
        for dq in (-1, 0, 1):
            for t in range(2):
                lane = slice(128 * t, 128 * t + 128)
                if dq == 0:
                    turned[0:size, lane] = full[t]
                elif dq < 0:
                    turned[1:size, lane] = full[t, 0 : size - 1, :]
                    turned[0:1, lane] = full[t, 0:1, :]
                else:
                    turned[0 : size - 1, lane] = full[t, 1:size, :]
                    turned[size - 1 : size, lane] = full[t, 0:1, :]
            for k, (dp, dq_k) in enumerate(AROUND):
                if dq_k == dq:
                    lhs = turned[48 * (1 + dp) : 48 * (1 + dp) + 48 * n, :]
                    total = total + couple(lhs, (inner_ref,), level, k)
        out[...] = total
        start += 6 * (n + 2)


def lane_of(f):
    return (f % 3) * 128 + (f // 3) * 64


def select(chosen, table):
    high, low = in_two(table)
    return dot(chosen, high) + dot(chosen, low)


def far_above(pos_ref, all_ref, pairs, transfer_ref, by_child, grown, side_by):
    gx, gy = pos_ref[0], pos_ref[1]
    table = jnp.concatenate([all_ref[pl.ds(m, 256, stride=4), :] for m in range(3)], axis=1)
    classes = table
    row = lax.broadcasted_iota(jnp.int32, (32, 1), 0)
    around, child = row % 8, row // 8
    shift_p = sum(jnp.where(around == k, dp, 0) for k, (dp, _) in enumerate(AROUND))
    shift_q = sum(jnp.where(around == k, dq, 0) for k, (_, dq) in enumerate(AROUND))
    outs = []
    for step in range(3):
        n = 16 >> step
        at_p, at_q = (gx >> (step + 1)) + shift_p, (gy >> (step + 1)) + shift_q
        inside = (at_p >= 0) & (at_p < n // 2) & (at_q >= 0) & (at_q < n // 2)
        if step == 0:
            where = child * (n * n // 4) + at_p * (n // 2) + at_q
        else:
            where = (2 * at_p + child // 2) * n + 2 * at_q + child % 2
        lane = lax.broadcasted_iota(jnp.int32, (32, n * n), 1)
        chosen = ((lane == where) & inside).astype(F32).astype(BF16)
        picked = select(chosen, table)
        by_child[...] = jnp.zeros(by_child.shape, F32)
        for f in range(6):
            for k in range(4):
                by_child[k // 2, 8 * f : 8 * f + 8, 64 * (k % 2) : 64 * (k % 2) + 64] = picked[
                    8 * k : 8 * k + 8, lane_of(f) : lane_of(f) + 64
                ]
        total = jnp.zeros((8, 256), F32)
        for k in range(8):
            lhs = tiles(by_child, pl.ds(k, 8, stride=8))
            total = total + couple(lhs, pairs, step, k)
        outs.append(total)
        if step == 2:
            break
        m = n * n // 4
        if step == 1:
            r = lax.broadcasted_iota(jnp.int32, (n * n, 1), 0)
            k, p, q = r // m, (r % m) // (n // 2), r % (n // 2)
            from_row = (2 * p + k // 2) * n + 2 * q + k % 2
            lane = lax.broadcasted_iota(jnp.int32, (n * n, n * n), 1)
            classes = select((lane == from_row).astype(F32).astype(BF16), table)
        for f in range(6):
            for k in range(4):
                side_by[m * f : m * f + m, 64 * k : 64 * k + 64] = classes[
                    m * k : m * k + m, lane_of(f) : lane_of(f) + 64
                ]
        lifted = jnp.dot(
            side_by[0 : 6 * m, :],
            transfer_ref[3 + step],
            precision=EXACT,
            preferred_element_type=F32,
        )
        for f in range(6):
            grown[0:m, lane_of(f) : lane_of(f) + 64] = lifted[m * f : m * f + m, :]
        table = grown[0:m, :]

    def own_child(x, step):
        bit_x, bit_y = (gx >> step) & 1, (gy >> step) & 1
        rows = [x[:, 64 * k : 64 * k + 64] for k in range(4)]
        low = jnp.where(bit_y == 1, rows[1], rows[0])
        high = jnp.where(bit_y == 1, rows[3], rows[2])
        return jnp.where(bit_x == 1, high, low)

    reached = own_child(outs[2], 2)
    for step in (1, 0):
        reached = own_child(outs[step] + dot_t(reached, transfer_ref[3 + step], EXACT), step)
    return jnp.concatenate([reached, jnp.zeros((8, 64), F32)], axis=1)


def far_down(reached, inner_ref, transfer_ref, flat, held):
    o0, o1, o2 = inner_parts(inner_ref)
    half = left_half((6, 128))
    flat[...] = jnp.zeros(flat.shape, F32)
    flat[pl.ds(1, 8, stride=8), :] = reached
    for level, out in ((2, o2), (1, o1), (0, o0)):
        n = PARENTS[level]
        value = out[...] + dot_t(flat[0 : 48 * n, :], doubled(transfer_ref[level]), EXACT)
        for t in range(2):
            held[t, 0 : 48 * n, :] = value[:, 128 * t : 128 * t + 128]
        offset = min(level, 1)
        for i in range(2 * n):
            for q in range(n):
                both = held[i % 2, pl.ds((i // 2) * 48 + 1 + q, 6, stride=8), :]
                at = 48 * i + offset + 2 * q
                flat[pl.ds(at, 6, stride=8), :] = jnp.where(half, both, 0.0)
                flat[pl.ds(at + 1, 6, stride=8), :] = jnp.where(half, 0.0, both)


def image_rows(i, flat, basis_ref, near_ref):
    d = flat[48 * i : 48 * i + 48, :]
    high = d.astype(BF16)
    low = (d - high.astype(F32)).astype(BF16)
    basis = jnp.concatenate([basis_ref[...]] * 4, axis=0)
    far = dot(jnp.concatenate([high, low], axis=1), basis)
    return near_ref[48 * i : 48 * i + 48, :] + far


def per_row(totals, slot):
    lane = lax.broadcasted_iota(jnp.int32, (1, 128), 1)
    field = lax.broadcasted_iota(jnp.int32, (48, 1), 0) // 8
    out = jnp.zeros((48, 1), F32)
    for f in range(6):
        out = out + jnp.where(
            field == f, jnp.sum(jnp.where(lane == 6 * slot + f, totals, 0.0)), 0.0
        )
    return out


FAR_SCRATCH = [
    pltpu.VMEM((2, 64, 128), F32),
    pltpu.VMEM((64, 384), F32),
    pltpu.VMEM((384, 256), F32),
    pltpu.VMEM((384, 128), F32),
    pltpu.VMEM((2, 192, 128), F32),
]


def second_source(
    pos_ref, all_ref, x_ref, near_ref, inner_ref, high_ref, low_ref, contrast_ref, occupied_ref, basis_ref,
    transfer_ref, u_ref, *rest,
):
    outs, (by_child, grown, side_by, flat, held, skel) = rest[:5], rest[5:]
    reached = far_above(pos_ref, all_ref, (high_ref, low_ref), transfer_ref, by_child, grown, side_by)
    far_down(reached, inner_ref, transfer_ref, flat, held)
    cross = jnp.zeros((48, 128), F32)
    square = jnp.zeros((48, 128), F32)
    for i in range(8):
        u = image_rows(i, flat, basis_ref, near_ref)
        u_ref[48 * i : 48 * i + 48, :] = u
        cross = cross + lanes_to_one(u * x_ref[48 * i : 48 * i + 48, :])
        square = square + lanes_to_one(u * u)
    spread_skeleton(
        lambda i: u_ref[48 * i : 48 * i + 48, :],
        field_row([cross, square]),
        ((contrast_ref, occupied_ref, basis_ref, transfer_ref), outs),
        skel,
    )


def scales(first_totals, second_totals, count):
    s = per_row(first_totals, 0) / count
    beta = jnp.sqrt(s + EPSILON)
    off_one = EPSILON / (s + EPSILON)
    one = s / (s + EPSILON)
    p = per_row(second_totals, 0) / count / (s + EPSILON)
    q = per_row(second_totals, 1) / count / (s + EPSILON)
    r = q + (off_one - p) * ((off_one - p) * one + 2.0 * p)
    h21 = jnp.sqrt(r + EPSILON)
    h11 = one + p
    return dict(
        beta=beta, h11=h11, h21=h21, lean=off_one - p, one=one,
        f12=off_one * h11 / h21, n2=r / (r + EPSILON), off_two=EPSILON / (r + EPSILON),
    )


def totals_of(all_ref):
    return jnp.sum(all_ref[pl.ds(3, 256, stride=4), :], axis=0, keepdims=True)


def last_sums(
    count, pos_ref, all_ref, before_ref, x_ref, u_ref, near_ref, inner_ref, high_ref, low_ref, basis_ref,
    transfer_ref, v_ref, sums_ref, totals_ref, by_child, grown, side_by, flat, held,
):
    first_totals, second_totals = totals_of(before_ref), totals_of(all_ref)
    totals_ref[0:1, :] = first_totals
    totals_ref[1:2, :] = second_totals
    k = scales(first_totals, second_totals, count)
    over, over_two = 1.0 / k["beta"], 1.0 / k["h21"]
    reached = far_above(pos_ref, all_ref, (high_ref, low_ref), transfer_ref, by_child, grown, side_by)
    far_down(reached, inner_ref, transfer_ref, flat, held)
    sums = [jnp.zeros((48, 128), F32)] * 3
    for i in range(8):
        rows = slice(48 * i, 48 * i + 48)
        first = x_ref[rows, :] * over
        image = u_ref[rows, :] * over
        second = (k["lean"] * first + image) * over_two
        v = (k["lean"] * image + image_rows(i, flat, basis_ref, near_ref) * over) * over_two
        v_ref[rows, :] = v
        sums = [
            s + lanes_to_one(w * v) for s, w in zip(sums, (first, second, v))
        ]
    lane = lax.broadcasted_iota(jnp.int32, (1, 128), 1)
    row = jnp.zeros((1, 128), F32)
    for n, acc in enumerate(sums):
        for f in range(6):
            row = row + jnp.where(lane == 16 * n + f, jnp.sum(acc[8 * f : 8 * f + 8, :]), 0.0)
    sums_ref[...] = jnp.broadcast_to(row[None], sums_ref.shape)


def finish(count, sums_ref, totals_ref, x_ref, u_ref, v_ref, third_ref, hess_ref, table):
    k = scales(totals_ref[0:1, :], totals_ref[1:2, :], count)
    total = jnp.sum(sums_ref[...], axis=0, keepdims=True) / count
    lane = lax.broadcasted_iota(jnp.int32, (1, 128), 1)
    field = lax.broadcasted_iota(jnp.int32, (48, 1), 0) // 8

    def rows_of(n):
        out = jnp.zeros((48, 1), F32)
        for f in range(6):
            out = out + jnp.where(
                field == f, jnp.sum(jnp.where(lane == 16 * n + f, total, 0.0)), 0.0
            )
        return out

    c1, c2, t = rows_of(0), rows_of(1), rows_of(2)
    h12, h22 = k["f12"] + c1, k["n2"] + c2
    g = k["off_two"] - c2
    rest = (
        t + g * g * k["n2"] + h12 * h12 * k["one"] + 2.0 * g * c2
        - 2.0 * h12 * c1 - 2.0 * g * h12 * k["f12"]
    )
    h32 = jnp.sqrt(rest + EPSILON)
    over, over_two, over_three = 1.0 / k["beta"], 1.0 / k["h21"], 1.0 / h32
    for i in range(8):
        rows = slice(48 * i, 48 * i + 48)
        first = x_ref[rows, :] * over
        second = (k["lean"] * first + u_ref[rows, :] * over) * over_two
        third_ref[rows, :] = (v_ref[rows, :] + g * second - h12 * first) * over_three
    lane48 = lax.broadcasted_iota(jnp.int32, (48, 128), 1)
    out = jnp.zeros((48, 128), F32)
    for n, h in enumerate((k["beta"], k["h11"], k["h21"], h12, h22, h32)):
        out = out + jnp.where(lane48 == n, h, 0.0)
    table[...] = out
    hess_ref[...] = table[pl.ds(0, 6, stride=8), :][:, 0:6]


def turn(n, s):
    return [(i, (i + s) % n) for i in range(n)]


def to_everyone(blocks):
    return lax.all_to_all(blocks, CLASS_ORDER, 0, 0, tiled=True)


def body(rhs, contrast, occupied, near, basis, transfer, coupling):
    side, _, fields, comps, voxels = rhs.shape
    count = float(128 * 128 * comps * voxels)
    x = rhs.transpose(0, 2, 1, 3, 4).reshape(384, 768)
    contrast = contrast.reshape(64, voxels)
    stacked = transfer.reshape(5, 256, 64)
    basis = basis.T
    pos = jnp.stack([lax.axis_index(GX), lax.axis_index(GY)]).astype(jnp.int32)
    shape = jax.ShapeDtypeStruct
    blocks = shape((3, 4, 256, 256), BF16)
    (inner,) = call(
        functools.partial(pair_blocks, 0), [blocks], [VMEM], [], 10**8, coupling
    )
    outer = call(
        functools.partial(pair_blocks, 3), [blocks] * 2, [VMEM], [], 10**8, coupling
    )

    def exchange(outs, inner):
        src, up, down, pay, tree = outs
        src, inner = lax.optimization_barrier((src, inner))
        above = lax.ppermute(up, GX, turn(16, 1))
        below = lax.ppermute(down, GX, turn(16, -1))
        to_left, to_right = call(
            columns, [shape((80, 1024), BF16)] * 2, [SMEM] + [VMEM] * 4,
            [pltpu.VMEM((12, 48, 128), F32)] * 2, 10**6,
            pos, src, tree, above, below,
        )
        pay, to_left, to_right = lax.optimization_barrier((pay, to_left, to_right))
        right = lax.ppermute(to_left, GY, turn(16, -1))
        left = lax.ppermute(to_right, GY, turn(16, 1))
        everyone = to_everyone(pay).reshape(1024, 128)
        parts = call(
            near_and_low,
            [shape((384, 768), F32), shape((336, 256), F32)],
            [SMEM] + [VMEM] * 6 + [pl.BlockSpec(memory_space=pl.ANY), VMEM],
            [
                pltpu.VMEM((5, 768, 768), BF16), pltpu.SemaphoreType.DMA((5,)),
                pltpu.VMEM((6, 480, 128), F32), pltpu.VMEM((6, 480, 128), F32), pltpu.VMEM((80, 768), F32),
                pltpu.VMEM((480, 768), BF16), pltpu.VMEM((2, 288, 128), F32), pltpu.VMEM((2, 192, 128), F32),
                pltpu.VMEM((2, 144, 128), F32), pltpu.VMEM((288, 256), F32),
            ],
            10**10,
            pos, src, tree, above, below, left, right, near, inner,
        )
        return everyone, parts

    outs = call(
        first_source, SOURCE_OUTS, [VMEM] * 5, SOURCE_SCRATCH, 10**8,
        x, contrast, occupied, basis, stacked,
    )
    all_one, parts = exchange(outs, inner)
    u, *outs = call(
        second_source, [shape((384, 768), F32)] + SOURCE_OUTS, [SMEM] + [VMEM] * 10,
        FAR_SCRATCH + SOURCE_SCRATCH, 10**8,
        pos, all_one, x, *parts, *outer, contrast, occupied, basis, stacked,
    )
    all_two, parts = exchange(outs, inner)
    v, sums, totals = call(
        functools.partial(last_sums, count),
        [shape((384, 768), F32), shape((256, 1, 128), F32), shape((8, 128), F32)],
        [SMEM] + [VMEM] * 10, FAR_SCRATCH, 10**8,
        pos, all_two, all_one, x, u, *parts, *outer, basis, stacked,
    )
    third, hess = call(
        functools.partial(finish, count),
        [shape((384, 768), F32), shape((6, 6), F32)], [VMEM] * 5, [pltpu.VMEM((48, 128), F32)], 10**6,
        to_everyone(sums).reshape(256, 128), totals, x, u, v,
    )
    third = third.reshape(side, fields, side, comps, voxels).transpose(0, 2, 1, 3, 4)
    return third, hess


def solution(mesh):
    grid = Mesh(mesh.devices.reshape(8, 2, 4, 2, 2), EVERYONE)
    placed = (P(GX, GY, None, None, None), P(GX, GY, None), P(GX, GY), P(), P(), P(), P())
    return jax.shard_map(
        body, mesh=grid, in_specs=placed,
        out_specs=(P(GX, GY, None, None, None), P()), check_vma=False,
    )
```
